256 devices in a mesh: row: 2 (over core), col: 4 (over x), depth: 32 (over z, y).
Axes of the slice: x: 4, y: 4, z: 8, core: 2. Of those that a mesh axis runs over, the one named last changes fastest.
Arguments:
- act_forward: bfloat16 [8192, 4096], P(('depth', 'col'), 'row'), may hold values from -6 to 6
- weight: bfloat16 [4096, 14336], P('row', 'col'), may hold values from -0.09375 to 0.09375
- act_backward: bfloat16 [8192, 4096], P(('depth', 'col'), 'row'), may hold values from -6 to 6
- pre_backward: bfloat16 [8192, 14336], P(('depth', 'row'), 'col'), may hold values from -8 to 8
- grad_backward: bfloat16 [8192, 14336], P(('depth', 'row'), 'col'), may hold values from -6 to 6
Outputs:
- hidden_forward: bfloat16 [8192, 14336], P(('depth', 'row'), 'col')
- grad_inputs: bfloat16 [8192, 4096], P(('depth', 'col'), 'row')
- grad_weight: float32 [4096, 14336], P('row', ('col', 'depth'))
The draws below stay inside these ranges and needn't reach their ends.
All inputs are finite; a program needn't handle non-finite values.
Results may differ from the reference program's by a relative error of at most 0.02.
Values may be sent and summed in bfloat16 or wider, within the bound.
No kernel may reach another device: no remote copies, remote signals or barrier semaphores. Data moves between devices by JAX's collectives and lax.ppermute only.
A program may use at most 128 MiB of HBM per device.

```python
import math
import jax
import jax.numpy as jnp

D = 4096
FF = 14336
TOK_DEP = 256
TOKENS = 8192
N_ROW = 2
N_DEPTH = 32


def shard_levels(key, extent, shards, least, top_value):
    loudness, own = 1.0, jax.random.fold_in(key, 6)
    for dim, blocks in shards:
        heights = jnp.exp(jax.random.uniform(jax.random.fold_in(own, dim), (blocks,), jnp.float32, least / len(shards), top_value / len(shards)))
        loudness = loudness * jnp.repeat(heights, extent[dim] // blocks).reshape([-1 if axis == dim else 1 for axis in range(len(extent))])
    return loudness


def noise(own_key, shape, width, most, shards=(), kind=jnp.bfloat16):
    array = jax.random.normal(own_key, shape, jnp.float32) * width
    if len(shards) > 0:
        array = shard_levels(own_key, shape, shards, -0.22, 0.18) * array
    return jnp.clip(array, min=-most, max=most).astype(kind)


def setup_inputs(seed: int = 0) -> dict:
    streams_of = jax.random.split(jax.random.key(seed), 6)
    act_forward = noise(streams_of[0], (TOKENS, D), 1.0, 6.0, ((0, 128), (1, 2)))
    weight = noise(streams_of[1], (D, FF), D ** -0.5, 0.09375, ((0, 2), (1, 4)))
    act_backward = noise(streams_of[2], (TOKENS, D), 1.0, 6.0, ((0, 128), (1, 2)))
    pre_backward = noise(streams_of[3], (TOKENS, FF), 1.5, 8.0, ((0, 64), (1, 4)))
    grad_backward = noise(streams_of[4], (TOKENS, FF), 1.0, 6.0, ((0, 64), (1, 4)))
    return dict(act_forward=act_forward, weight=weight, act_backward=act_backward, pre_backward=pre_backward, grad_backward=grad_backward)


coeff = math.sqrt(2.0 / math.pi)

def gelu_value(v):
    inner = coeff * (v + 0.044715 * v * v * v)
    return 0.5 * v * (1.0 + jnp.tanh(inner))

def gelu_slope(v):
    tanh_part = jnp.tanh(coeff * (v + 0.044715 * v * v * v))
    return 0.5 * (1.0 + tanh_part) + 0.5 * v * (1.0 - tanh_part * tanh_part) * coeff * (1.0 + 3.0 * 0.044715 * v * v)

def reference(act_forward, weight, act_backward, pre_backward, grad_backward):
    block = D // N_ROW
    pre_forward = jnp.zeros((act_forward.shape[0], FF), jnp.float32)
    for index in range(N_ROW):
        part = jnp.dot(act_forward[:, index * block:(index + 1) * block], weight[index * block:(index + 1) * block, :], preferred_element_type=jnp.float32)
        pre_forward = pre_forward + part.astype(jnp.bfloat16).astype(jnp.float32)
    hidden_forward = gelu_value(pre_forward).astype(jnp.bfloat16)
    grad_pre = (grad_backward.astype(jnp.float32) * gelu_slope(pre_backward.astype(jnp.float32))).astype(jnp.bfloat16)
    grad_inputs = jnp.dot(grad_pre, weight.T, preferred_element_type=jnp.float32).astype(jnp.bfloat16)
    grad_weight = jnp.zeros((D, FF), jnp.float32)
    for group in range(N_DEPTH):
        rows_in = act_backward[group * TOK_DEP:(group + 1) * TOK_DEP, :]
        rows_grad = grad_pre[group * TOK_DEP:(group + 1) * TOK_DEP, :]
        part = jnp.dot(rows_in.T, rows_grad, preferred_element_type=jnp.float32)
        grad_weight = grad_weight + part.astype(jnp.bfloat16).astype(jnp.float32)
    return (hidden_forward, grad_inputs, grad_weight)
```

```python
import math

import jax
import jax.numpy as jnp
from jax import lax
from jax.experimental import pallas as pl
from jax.experimental.pallas import tpu as pltpu
from jax.sharding import Mesh, PartitionSpec as P

coeff = math.sqrt(2.0 / math.pi)
BF = jnp.bfloat16
F32 = jnp.float32
SIZES = {"row": 2, "col": 4, "z": 8, "y": 4}


def gelu_value(v):
    inner = coeff * (v + 0.044715 * v * v * v)
    return 0.5 * v * (1.0 + jnp.tanh(inner))


def gelu_slope(v):
    tanh_part = jnp.tanh(coeff * (v + 0.044715 * v * v * v))
    return 0.5 * (1.0 + tanh_part) + 0.5 * v * (1.0 - tanh_part * tanh_part) * coeff * (
        1.0 + 3.0 * 0.044715 * v * v
    )


def send(value, axis, step):
    n = SIZES[axis]
    return lax.ppermute(value, axis, [(i, (i + step) % n) for i in range(n)])


def grad_kernel(pre_ref, grad_ref, out_ref, flip_ref):
    g = grad_ref[...].astype(F32) * gelu_slope(pre_ref[...].astype(F32))
    out_ref[...] = g.astype(BF)
    flip_ref[...] = g.T.astype(BF)


def grad_pre_both(pre, grad):
    rows, cols = pre.shape
    tile = 512
    return pl.pallas_call(
        grad_kernel,
        grid=(cols // tile,),
        in_specs=[pl.BlockSpec((rows, tile), lambda i: (0, i))] * 2,
        out_specs=[
            pl.BlockSpec((rows, tile), lambda i: (0, i)),
            pl.BlockSpec((tile, rows), lambda i: (i, 0)),
        ],
        out_shape=[
            jax.ShapeDtypeStruct((rows, cols), BF),
            jax.ShapeDtypeStruct((cols, rows), BF),
        ],
        compiler_params=pltpu.CompilerParams(vmem_limit_bytes=16 * 2**20),
        cost_estimate=pl.CostEstimate(
            flops=30 * rows * cols, bytes_accessed=8 * rows * cols, transcendentals=rows * cols
        ),
    )(pre, grad)


def part_kernel(place_ref, own_ref, oth_ref, b0, b1, b2, b3, out_ref, acts):
    @pl.when(pl.program_id(0) == 0)
    def _():
        x, r = place_ref[0], place_ref[1]
        for d, block in enumerate((b0, b1, b2, b3)):
            at = lax.rem(x + d, 4)
            start = ((at // 2) ^ r) * 512 + lax.rem(at, 2) * 64
            for j in range(4):
                rows = pl.ds(pl.multiple_of(start + j * 128, 64), 64)
                acts[rows, :] = block[j * 64 : (j + 1) * 64, :]

    total = jnp.dot(own_ref[...], acts[0:512, :], preferred_element_type=F32)
    total += jnp.dot(oth_ref[...], acts[512:1024, :], preferred_element_type=F32)
    out_ref[...] = total.astype(BF)


def weight_part(place, own, oth, blocks):
    rows, wide = own.shape[0], blocks[0].shape[1]
    tile = 256
    whole = pl.BlockSpec((256, wide), lambda i, s: (0, 0))
    return pl.pallas_call(
        part_kernel,
        grid_spec=pltpu.PrefetchScalarGridSpec(
            num_scalar_prefetch=1,
            grid=(rows // tile,),
            in_specs=[pl.BlockSpec((tile, 512), lambda i, s: (i, 0))] * 2 + [whole] * 4,
            out_specs=pl.BlockSpec((tile, wide), lambda i, s: (i, 0)),
            scratch_shapes=[pltpu.VMEM((1024, wide), BF)],
        ),
        out_shape=jax.ShapeDtypeStruct((rows, wide), BF),
        compiler_params=pltpu.CompilerParams(vmem_limit_bytes=24 * 2**20),
        cost_estimate=pl.CostEstimate(
            flops=2 * rows * 1024 * wide, bytes_accessed=2 * rows * (1024 + wide), transcendentals=0
        ),
    )(place, own, oth, *blocks)


def reduce_z(part, z, step):
    def piece(offset):
        return lax.dynamic_index_in_dim(part, (z + offset) % 8, 0, keepdims=False)

    far, near = piece(4), piece(-3 * step)
    for hop in (3, 2, 1, 0):
        far = send(far, "z", step)
        if hop >= 1:
            near = send(near, "z", -step)
            far = far + piece(hop * step)
            if hop > 1:
                near = near + piece(-(hop - 1) * step)
    return piece(0).astype(F32) + far.astype(F32) + near.astype(F32)


def on_device(act_forward, weight, act_backward, pre_backward, grad_backward):
    r, x, z, y = (lax.axis_index(name) for name in ("row", "col", "z", "y"))
    ym, yn = y % 2, y // 2
    place = jnp.stack([x, r]).astype(jnp.int32)

    same = lax.dynamic_slice(act_backward, (0, ym * 1024), (64, 1024))
    other = lax.dynamic_slice(act_backward, (0, (1 - ym) * 1024), (64, 1024))
    acts = [same, send(other, "y", 1), send(other, "y", -1), send(same, "y", 2)]

    fwd = [
        act_forward,
        send(act_forward, "col", -1),
        send(act_forward, "col", 2),
        send(act_forward, "col", 1),
    ]

    grad_pre, flipped = grad_pre_both(pre_backward, grad_backward)
    flipped = flipped.reshape(8, 2, 224, 128)

    def hidden_half(which):
        return lax.dynamic_index_in_dim(flipped, which, 1, keepdims=False).reshape(1792, 128)

    grads = [
        hidden_half(yn),
        send(hidden_half(((y + 1) % 4) // 2), "y", 1),
        send(hidden_half(((y + 3) % 4) // 2), "y", -1),
        send(hidden_half(1 - yn), "y", 2),
    ]
    grads_own = jnp.concatenate(grads, axis=1)
    grads_other = send(grads_own, "row", 1)

    acts = jnp.concatenate(acts, axis=0)
    sums = []
    for c in range(2):
        mine = acts[:, c * 512 : (c + 1) * 512]
        blocks = (mine, send(mine, "col", -1), send(mine, "col", 2), send(mine, "col", 1))
        part = weight_part(place, grads_own, grads_other, blocks).reshape(8, 224, 512)
        sums.append(reduce_z(part, z, 1 - 2 * c))
    total = jnp.concatenate(sums, axis=1).reshape(2, 112, 1024)
    kept = lax.dynamic_index_in_dim(total, ym, 0, keepdims=False)
    given = lax.dynamic_index_in_dim(total, 1 - ym, 0, keepdims=False).astype(BF)
    got = lax.ppermute(given, "y", [(0, 1), (1, 0), (2, 3), (3, 2)]).astype(F32)
    grad_weight = jnp.where(
        ym == 0, jnp.concatenate([kept, got], axis=1), jnp.concatenate([got, kept], axis=1)
    ).T

    rows_fwd = jnp.zeros((256, 2048), BF)
    for d, block in enumerate(fwd):
        at = (x + d) % 4
        rows_fwd = lax.dynamic_update_slice(
            rows_fwd, block, (((at // 2) ^ r) * 128 + (at % 2) * 64, 0)
        )
    part_fwd = jnp.dot(rows_fwd, weight, preferred_element_type=F32).astype(BF)
    pre_forward = part_fwd[:128].astype(F32) + send(part_fwd[128:], "row", 1).astype(F32)
    hidden_forward = gelu_value(pre_forward).astype(BF)

    grad_full = jnp.concatenate([grad_pre, send(grad_pre, "row", 1)], axis=0)
    part_in = lax.dot_general(
        grad_full, weight, (((1,), (1,)), ((), ())), preferred_element_type=F32
    ).astype(BF)

    def tokens_of(offset):
        at = (x + offset) % 4
        return lax.dynamic_slice(part_in, (((at // 2) ^ r) * 128 + (at % 2) * 64, 0), (64, 2048))

    grad_inputs = (
        tokens_of(0).astype(F32)
        + send(tokens_of(1), "col", 1).astype(F32)
        + send(tokens_of(3), "col", -1).astype(F32)
        + send(tokens_of(2), "col", 2).astype(F32)
    ).astype(BF)
    return hidden_forward, grad_inputs, grad_weight


def solution(mesh):
    fine = Mesh(mesh.devices.reshape(2, 4, 8, 4), ("row", "col", "z", "y"))
    in_specs = (
        P(("z", "y", "col"), "row"),
        P("row", "col"),
        P(("z", "y", "col"), "row"),
        P(("z", "y", "row"), "col"),
        P(("z", "y", "row"), "col"),
    )
    out_specs = (
        P(("z", "y", "row"), "col"),
        P(("z", "y", "col"), "row"),
        P("row", ("col", "z", "y")),
    )
    return jax.shard_map(
        on_device, mesh=fine, in_specs=in_specs, out_specs=out_specs, check_vma=False
    )
```

```python
import functools
import math

import jax
import jax.numpy as jnp
from jax import lax
from jax.experimental import pallas as pl
from jax.experimental.pallas import tpu as pltpu
from jax.sharding import Mesh, PartitionSpec as P

coeff = math.sqrt(2.0 / math.pi)
BF = jnp.bfloat16
F32 = jnp.float32
SIZES = {"row": 2, "col": 4, "z": 8, "y": 4}


def gelu_value(v):
    inner = coeff * (v + 0.044715 * v * v * v)
    return 0.5 * v * (1.0 + jnp.tanh(inner))


def gelu_slope(v):
    tanh_part = jnp.tanh(coeff * (v + 0.044715 * v * v * v))
    return 0.5 * (1.0 + tanh_part) + 0.5 * v * (1.0 - tanh_part * tanh_part) * coeff * (
        1.0 + 3.0 * 0.044715 * v * v
    )


def send(value, axis, step):
    n = SIZES[axis]
    return lax.ppermute(value, axis, [(i, (i + step) % n) for i in range(n)])


def together(*values):
    return lax.optimization_barrier(values)


VMEM = pl.BlockSpec(memory_space=pltpu.VMEM)
SMEM = pl.BlockSpec(memory_space=pltpu.SMEM)


def params(mib):
    return pltpu.CompilerParams(vmem_limit_bytes=mib * 2**20)


def grad_kernel(pre_ref, grad_ref, flip_ref, parts_ref):
    g = grad_ref[...].astype(F32) * gelu_slope(pre_ref[...].astype(F32))
    flip = g.T.astype(BF)
    flip_ref[...] = flip
    for k in range(2):
        for q in range(4):
            block = flip[k * 448 + q * 112 : k * 448 + q * 112 + 112]
            parts_ref[q ^ 1, 0, k * 112 : k * 112 + 112] = block
            parts_ref[q, 1, k * 112 : k * 112 + 112] = block


def grad_pre_flipped(pre, grad):
    rows, cols = pre.shape
    tile = 896
    return pl.pallas_call(
        grad_kernel,
        grid=(cols // tile,),
        in_specs=[pl.BlockSpec((rows, tile), lambda i: (0, i))] * 2,
        out_specs=[
            pl.BlockSpec((tile, rows), lambda i: (i, 0)),
            pl.BlockSpec((4, 2, tile // 4, rows), lambda i: (0, 0, i, 0)),
        ],
        out_shape=[
            jax.ShapeDtypeStruct((cols, rows), BF),
            jax.ShapeDtypeStruct((4, 2, cols // 4, rows), BF),
        ],
        compiler_params=params(60),
        cost_estimate=pl.CostEstimate(
            flops=30 * rows * cols, bytes_accessed=10 * rows * cols, transcendentals=rows * cols
        ),
    )(pre, grad)


def copy_acts(place_ref, blocks, acts, sems):
    x, r, y = place_ref[0], place_ref[1], place_ref[2]
    copies = []
    for d, block in enumerate(blocks):
        at = lax.rem(x + d, 4)
        start = ((at // 2) ^ r) * 512 + lax.rem(at, 2) * 64
        for j, turn in enumerate((0, 3, 1, 2)):
            row = pl.multiple_of(start + lax.rem(y + turn, 4) * 128, 64)
            copies.append((block.at[pl.ds(j * 64, 64), :], acts.at[pl.ds(row, 64), :]))
    return [pltpu.make_async_copy(a, b, sems.at[n]) for n, (a, b) in enumerate(copies)]


def first_kernel(wanted, place_ref, own_ref, oth_ref, b0, b1, b2, b3, *rest):
    outs, (acts, lhs, sems) = rest[:-3], rest[-3:]
    z = place_ref[3]
    copies = copy_acts(place_ref, (b0, b1, b2, b3), acts, sems)
    for i, (which, offset) in enumerate(wanted):
        rows = pl.ds(pl.multiple_of(lax.rem(z + offset, 8) * 112, 16), 112)
        for h, ref in enumerate((own_ref, oth_ref)):
            for k in range(4):
                to = lhs.at[pl.ds(i * 112, 112), pl.ds(h * 512 + k * 128, 128)]
                sem = sems.at[len(copies)]
                copies.append(pltpu.make_async_copy(ref.at[k, which, rows, :], to, sem))
    for copy in copies:
        copy.start()
    for copy in copies:
        copy.wait()
    part = jnp.dot(lhs[...], acts[...], preferred_element_type=F32)
    for i, out in enumerate(outs):
        out[...] = part[i * 112 : i * 112 + 112].astype(BF)


def rest_kernel(wanted, place_ref, own_ref, oth_ref, b0, b1, b2, b3, *rest):
    outs, (acts, lhs, sems) = rest[:-3], rest[-3:]
    z = place_ref[3]
    copies = copy_acts(place_ref, (b0, b1, b2, b3), acts, sems)
    for which in range(2):
        for h, ref in enumerate((own_ref, oth_ref)):
            for k in range(4):
                to = lhs.at[which, :, pl.ds(h * 512 + k * 128, 128)]
                copies.append(pltpu.make_async_copy(ref.at[k, which], to, sems.at[len(copies)]))
    for copy in copies:
        copy.start()
    for copy in copies:
        copy.wait()
    for i in range(0, len(wanted), 4):
        rows = [
            lhs[which, pl.ds(pl.multiple_of(lax.rem(z + offset, 8) * 112, 16), 112), :]
            for which, offset in wanted[i : i + 4]
        ]
        part = jnp.dot(jnp.concatenate(rows, axis=0), acts[...], preferred_element_type=F32)
        for k in range(4):
            outs[i + k][...] = part[k * 112 : k * 112 + 112].astype(BF)


def weight_parts(place, own, oth, blocks, wanted, first):
    anywhere = pl.BlockSpec(memory_space=pl.ANY)
    n = len(wanted)
    return pl.pallas_call(
        functools.partial(first_kernel if first else rest_kernel, wanted),
        grid=(1,),
        in_specs=[SMEM] + [anywhere] * 6,
        out_specs=[pl.BlockSpec((112, 1024), lambda i: (0, 0))] * n,
        scratch_shapes=[
            pltpu.VMEM((1024, 1024), BF),
            pltpu.VMEM((112 * n, 1024) if first else (2, 896, 1024), BF),
            pltpu.SemaphoreType.DMA((16 + (8 * n if first else 16),)),
        ],
        out_shape=[jax.ShapeDtypeStruct((112, 1024), BF)] * n,
        compiler_params=params(60),
        cost_estimate=pl.CostEstimate(flops=2**20, bytes_accessed=2**20, transcendentals=0),
    )(place, own, oth, *blocks)


def both_kernel(place_ref, f0, f1, f2, f3, own_ref, oth_ref, w_ref, keep_ref, give_ref, o0, o1, o2, o3, rows_ref, acc):
    step, last = pl.program_id(0), pl.num_programs(0) - 1
    x, r = place_ref[0], place_ref[1]

    @pl.when(step == 0)
    def _():
        for d, ref in enumerate((f0, f1, f2, f3)):
            at = lax.rem(x + d, 4)
            row = ((at // 2) ^ r) * 128 + lax.rem(at, 2) * 64
            rows_ref[pl.ds(pl.multiple_of(row, 64), 64), :] = ref[...]

    w = w_ref[...]
    part = jnp.dot(rows_ref[...], w, preferred_element_type=F32).astype(BF)
    keep_ref[...] = part[:128]
    give_ref[...] = part[128:]
    both = jnp.concatenate([own_ref[...], oth_ref[...]], axis=1)
    more = jnp.dot(w, both, preferred_element_type=F32)

    @pl.when(step == 0)
    def _():
        acc[...] = more

    @pl.when(step > 0)
    def _():
        acc[...] += more

    @pl.when(step == last)
    def _():
        flat = acc[...].T.astype(BF)
        rows_ref[...] = flat
        for d, out in enumerate((o0, o1, o2, o3)):
            at = lax.rem(x + d, 4)
            row = ((at // 2) ^ r) * 128 + lax.rem(at, 2) * 64
            out[...] = rows_ref[pl.ds(pl.multiple_of(row, 64), 64), :]


def both_products(place, fwd, own, oth, weight):
    feats, hidden = weight.shape
    tile = 512
    return pl.pallas_call(
        both_kernel,
        grid=(hidden // tile,),
        in_specs=[SMEM]
        + [pl.BlockSpec((64, feats), lambda i: (0, 0))] * 4
        + [pl.BlockSpec((tile, 128), lambda i: (i, 0))] * 2
        + [pl.BlockSpec((feats, tile), lambda i: (0, i))],
        out_specs=[pl.BlockSpec((128, tile), lambda i: (0, i))] * 2
        + [pl.BlockSpec((64, feats), lambda i: (0, 0))] * 4,
        out_shape=[jax.ShapeDtypeStruct((128, hidden), BF)] * 2
        + [jax.ShapeDtypeStruct((64, feats), BF)] * 4,
        scratch_shapes=[pltpu.VMEM((256, feats), BF), pltpu.VMEM((feats, 256), F32)],
        compiler_params=params(60),
        cost_estimate=pl.CostEstimate(
            flops=4 * 256 * 2048 * hidden, bytes_accessed=2 * 2048 * hidden, transcendentals=0
        ),
    )(place, *fwd, own, oth, weight)


def reduce_z(piece, step):
    far, near = piece[4], piece[-3 * step % 8]
    for hop in (3, 2, 1, 0):
        far = send(far, "z", step)
        if hop >= 1:
            near = send(near, "z", -step)
            far = far + piece[hop * step % 8]
            if hop > 1:
                near = near + piece[-(hop - 1) * step % 8]
    return piece[0].astype(F32) + far.astype(F32) + near.astype(F32)


def on_device(act_forward, weight, act_backward, pre_backward, grad_backward):
    r, x, z, y = (lax.axis_index(name) for name in ("row", "col", "z", "y"))
    ym = y % 2
    place = jnp.stack([x, r, y, z]).astype(jnp.int32)

    left, right = send(act_forward, "col", 1), send(act_forward, "col", -1)

    same = lax.dynamic_slice(act_backward, (0, ym * 1024), (64, 1024))
    other = lax.dynamic_slice(act_backward, (0, (1 - ym) * 1024), (64, 1024))
    acts = jnp.concatenate(
        [same, send(other, "y", 1), send(other, "y", -1), send(same, "y", 2)], axis=0
    )
    flipped, halves = grad_pre_flipped(pre_backward, grad_backward)

    acts, halves, left, right, act_forward = together(acts, halves, left, right, act_forward)
    far = send(act_forward, "col", 2)
    b1, b2, b3 = send(acts, "col", -1), send(acts, "col", 2), send(acts, "col", 1)
    flipped_other = send(flipped, "row", 1)
    grads_own = lax.all_to_all(halves, "y", 0, 0)
    keep, give, mine, to_right, to_far, to_left = both_products(
        place, (act_forward, right, far, left), flipped, flipped_other, weight
    )

    grads_own, give, b1, b2, b3 = together(grads_own, give, b1, b2, b3)
    pre_forward = keep.astype(F32) + send(give, "row", 1).astype(F32)
    hidden_forward = gelu_value(pre_forward).astype(BF)
    grads_other, hidden_forward = together(send(grads_own, "row", 1), hidden_forward)
    parts = {}
    first = [(0, 4), (0, 5), (1, 4), (1, 3)]
    others = [(w, o) for w in range(2) for o in range(8) if (w, o) not in first]
    for wanted in (first, others):
        got = weight_parts(
            place, grads_own, grads_other, (acts, b1, b2, b3), wanted, wanted is first
        )
        parts.update(zip(wanted, got))
    given, kept = ([parts[w, o] for o in range(8)] for w in range(2))
    given = reduce_z(given, 1).astype(BF)
    kept = reduce_z(kept, -1)
    grad_inputs = (
        mine.astype(F32)
        + send(to_right, "col", 1).astype(F32)
        + send(to_left, "col", -1).astype(F32)
        + send(to_far, "col", 2).astype(F32)
    ).astype(BF)
    got = lax.ppermute(given, "y", [(0, 1), (1, 0), (2, 3), (3, 2)]).astype(F32)
    grad_weight = jnp.where(
        ym == 0, jnp.concatenate([kept, got], axis=1), jnp.concatenate([got, kept], axis=1)
    ).T
    return hidden_forward, grad_inputs, grad_weight


def solution(mesh):
    fine = Mesh(mesh.devices.reshape(2, 4, 8, 4), ("row", "col", "z", "y"))
    in_specs = (
        P(("z", "y", "col"), "row"),
        P("row", "col"),
        P(("z", "y", "col"), "row"),
        P(("z", "y", "row"), "col"),
        P(("z", "y", "row"), "col"),
    )
    out_specs = (
        P(("z", "y", "row"), "col"),
        P(("z", "y", "col"), "row"),
        P("row", ("col", "z", "y")),
    )
    return jax.shard_map(
        on_device, mesh=fine, in_specs=in_specs, out_specs=out_specs, check_vma=False
    )
```

```python
import functools
import math

import jax
import jax.numpy as jnp
from jax import lax
from jax.experimental import pallas as pl
from jax.experimental.pallas import tpu as pltpu
from jax.sharding import Mesh, PartitionSpec as P

coeff = math.sqrt(2.0 / math.pi)
BF = jnp.bfloat16
F32 = jnp.float32
SIZES = {"row": 2, "col": 4, "z": 8, "y": 4}


def gelu_value(v):
    inner = coeff * (v + 0.044715 * v * v * v)
    return 0.5 * v * (1.0 + jnp.tanh(inner))


def gelu_slope(v):
    tanh_part = jnp.tanh(coeff * (v + 0.044715 * v * v * v))
    return 0.5 * (1.0 + tanh_part) + 0.5 * v * (1.0 - tanh_part * tanh_part) * coeff * (
        1.0 + 3.0 * 0.044715 * v * v
    )


def send(value, axis, step):
    n = SIZES[axis]
    return lax.ppermute(value, axis, [(i, (i + step) % n) for i in range(n)])


def together(*values):
    return lax.optimization_barrier(values)


VMEM = pl.BlockSpec(memory_space=pltpu.VMEM)
SMEM = pl.BlockSpec(memory_space=pltpu.SMEM)


def params(mib):
    return pltpu.CompilerParams(vmem_limit_bytes=mib * 2**20)


def grad_kernel(pre_ref, grad_ref, flip_ref, parts_ref):
    g = grad_ref[...].astype(F32) * gelu_slope(pre_ref[...].astype(F32))
    flip = g.T.astype(BF)
    flip_ref[...] = flip
    for k in range(2):
        for q in range(4):
            block = flip[k * 448 + q * 112 : k * 448 + q * 112 + 112]
            parts_ref[q ^ 1, 0, k * 112 : k * 112 + 112] = block
            parts_ref[q, 1, k * 112 : k * 112 + 112] = block


def grad_pre_flipped(pre, grad):
    rows, cols = pre.shape
    tile = 896
    return pl.pallas_call(
        grad_kernel,
        grid=(cols // tile,),
        in_specs=[pl.BlockSpec((rows, tile), lambda i: (0, i))] * 2,
        out_specs=[
            pl.BlockSpec((tile, rows), lambda i: (i, 0)),
            pl.BlockSpec((4, 2, tile // 4, rows), lambda i: (0, 0, i, 0)),
        ],
        out_shape=[
            jax.ShapeDtypeStruct((cols, rows), BF),
            jax.ShapeDtypeStruct((4, 2, cols // 4, rows), BF),
        ],
        compiler_params=params(60),
        cost_estimate=pl.CostEstimate(
            flops=30 * rows * cols, bytes_accessed=10 * rows * cols, transcendentals=rows * cols
        ),
    )(pre, grad)


def copy_acts(place_ref, blocks, acts, sems):
    x, r, y = (lax.axis_index(n) for n in ("col", "row", "y"))
    copies = []
    for d, block in enumerate(blocks):
        at = lax.rem(x + d, 4)
        start = ((at // 2) ^ r) * 512 + lax.rem(at, 2) * 64
        for j, turn in enumerate((0, 3, 1, 2)):
            row = pl.multiple_of(start + lax.rem(y + turn, 4) * 128, 64)
            copies.append((block.at[pl.ds(j * 64, 64), :], acts.at[pl.ds(row, 64), :]))
    return [pltpu.make_async_copy(a, b, sems.at[n]) for n, (a, b) in enumerate(copies)]


def first_kernel(wanted, place_ref, own_ref, oth_ref, b0, b1, b2, b3, *rest):
    outs, (acts, lhs, sems) = rest[:-3], rest[-3:]
    z = lax.axis_index("z")
    copies = copy_acts(place_ref, (b0, b1, b2, b3), acts, sems)
    for i, (which, offset) in enumerate(wanted):
        rows = pl.ds(pl.multiple_of(lax.rem(z + offset, 8) * 112, 16), 112)
        for h, ref in enumerate((own_ref, oth_ref)):
            for k in range(4):
                to = lhs.at[pl.ds(i * 112, 112), pl.ds(h * 512 + k * 128, 128)]
                sem = sems.at[len(copies)]
                copies.append(pltpu.make_async_copy(ref.at[k, which, rows, :], to, sem))
    for copy in copies:
        copy.start()
    for copy in copies:
        copy.wait()
    part = jnp.dot(lhs[...], acts[...], preferred_element_type=F32)
    for i, out in enumerate(outs):
        out[...] = part[i * 112 : i * 112 + 112].astype(BF)


def rest_kernel(wanted, place_ref, own_ref, oth_ref, b0, b1, b2, b3, *rest):
    outs, (acts, lhs, sems) = rest[:-3], rest[-3:]
    z = lax.axis_index("z")
    copies = copy_acts(place_ref, (b0, b1, b2, b3), acts, sems)
    for which in range(2):
        for h, ref in enumerate((own_ref, oth_ref)):
            for k in range(4):
                to = lhs.at[which, :, pl.ds(h * 512 + k * 128, 128)]
                copies.append(pltpu.make_async_copy(ref.at[k, which], to, sems.at[len(copies)]))
    for copy in copies:
        copy.start()
    for copy in copies:
        copy.wait()
    for i in range(0, len(wanted), 4):
        rows = [
            lhs[which, pl.ds(pl.multiple_of(lax.rem(z + offset, 8) * 112, 16), 112), :]
            for which, offset in wanted[i : i + 4]
        ]
        part = jnp.dot(jnp.concatenate(rows, axis=0), acts[...], preferred_element_type=F32)
        for k in range(4):
            outs[i + k][...] = part[k * 112 : k * 112 + 112].astype(BF)


def weight_parts(place, own, oth, blocks, wanted, first, late=()):
    anywhere = pl.BlockSpec(memory_space=pl.ANY)
    n = len(wanted)
    return pl.pallas_call(
        functools.partial(first_kernel if first else rest_kernel, wanted),
        grid=(1,),
        in_specs=[SMEM] + [anywhere] * (6 + len(late)),
        out_specs=[pl.BlockSpec((112, 1024), lambda i: (0, 0))] * n,
        scratch_shapes=[
            pltpu.VMEM((1024, 1024), BF),
            pltpu.VMEM((112 * n, 1024) if first else (2, 896, 1024), BF),
            pltpu.SemaphoreType.DMA((16 + (8 * n if first else 16),)),
        ],
        out_shape=[jax.ShapeDtypeStruct((112, 1024), BF)] * n,
        compiler_params=params(60),
        cost_estimate=pl.CostEstimate(flops=2**20, bytes_accessed=2**20, transcendentals=0),
    )(place, own, oth, *blocks, *late)


def both_kernel(place_ref, f0, f1, f2, f3, own_ref, oth_ref, w_ref, keep_ref, out_ref, *rest):
    gives, rows_ref, acc = rest[:-2], rest[-2], rest[-1]
    step, last = pl.program_id(0), pl.num_programs(0) - 1
    x, r = lax.axis_index("col"), lax.axis_index("row")

    @pl.when(step == 0)
    def _():
        for d, ref in enumerate((f0, f1, f2, f3)):
            at = lax.rem(x + d, 4)
            row = ((at // 2) ^ r) * 128 + lax.rem(at, 2) * 64
            rows_ref[pl.ds(pl.multiple_of(row, 64), 64), :] = ref[...]

    w = w_ref[...]
    part = jnp.dot(rows_ref[...], w, preferred_element_type=F32).astype(BF)
    keep_ref[...] = part[:128]
    for k, give in enumerate(gives):
        give[...] = part[128 + 64 * k : 192 + 64 * k]
    both = jnp.concatenate([own_ref[...], oth_ref[...]], axis=1)
    more = jnp.dot(w, both, preferred_element_type=F32)

    @pl.when(step == 0)
    def _():
        acc[...] = more

    @pl.when(step > 0)
    def _():
        acc[...] += more

    @pl.when(step == last)
    def _():
        flat = acc[...].T.astype(BF)
        for half in range(2):
            for k in range(2):
                at = (half ^ r) * 2 + k
                out_ref[at] = flat[half * 128 + k * 64 : half * 128 + k * 64 + 64]


def both_products(place, fwd, own, oth, weight):
    feats, hidden = weight.shape
    tile = 512
    return pl.pallas_call(
        both_kernel,
        grid=(hidden // tile,),
        in_specs=[SMEM]
        + [pl.BlockSpec((64, feats), lambda i: (0, 0))] * 4
        + [pl.BlockSpec((tile, 128), lambda i: (i, 0))] * 2
        + [pl.BlockSpec((feats, tile), lambda i: (0, i))],
        out_specs=[
            pl.BlockSpec((128, tile), lambda i: (0, i)),
            pl.BlockSpec((4, 64, feats), lambda i: (0, 0, 0)),
        ]
        + [pl.BlockSpec((64, tile), lambda i: (0, i))] * 2,
        out_shape=[
            jax.ShapeDtypeStruct((128, hidden), BF),
            jax.ShapeDtypeStruct((4, 64, feats), BF),
        ]
        + [jax.ShapeDtypeStruct((64, hidden), BF)] * 2,
        scratch_shapes=[pltpu.VMEM((256, feats), BF), pltpu.VMEM((feats, 256), F32)],
        compiler_params=params(60),
        cost_estimate=pl.CostEstimate(
            flops=12 * 256 * 2048 * hidden, bytes_accessed=2 * 2048 * hidden, transcendentals=0
        ),
    )(place, *fwd, own, oth, weight)


def gelu_kernel(keep_ref, *refs):
    out_ref, rows = refs[-1], refs[0].shape[0]
    for k, got in enumerate(refs[:-1]):
        at = pl.ds(k * rows, rows)
        v = keep_ref[at, :].astype(F32) + got[...].astype(F32)
        out_ref[at, :] = gelu_value(v).astype(BF)


def gelu_rows(keep, got):
    rows, cols = keep.shape
    tile = 896
    whole = pl.BlockSpec((rows, tile), lambda i: (0, i))
    return pl.pallas_call(
        gelu_kernel,
        grid=(cols // tile,),
        in_specs=[whole] + [pl.BlockSpec((rows // len(got), tile), lambda i: (0, i))] * len(got),
        out_specs=whole,
        out_shape=jax.ShapeDtypeStruct((rows, cols), BF),
        compiler_params=params(60),
        cost_estimate=pl.CostEstimate(flops=2**18, bytes_accessed=2**18, transcendentals=0),
    )(keep, *got)


def reduce_z(piece, step, swap, late=None):
    partner = [(k, k ^ 1) for k in range(4)]
    far, near = piece[4], piece[-3 * step % 8]
    for hop in (3, 2, 1):
        far = send(far, "z", step)
        if hop == 3 and late is not None:
            far, late = together(far, late)
        near = send(near, "z", -step)
        far = far + piece[hop * step % 8]
        if hop > 1:
            near = near + piece[-(hop - 1) * step % 8]
    if swap:
        near = lax.ppermute(near + piece[0], "y", partner)
        steps = [(k * 4 + a, (k + step) % 8 * 4 + b) for k in range(8) for a, b in partner]
        far = lax.ppermute(far, ("z", "y"), steps)
        return near.astype(F32) + far.astype(F32), late
    far = send(far, "z", step)
    return piece[0].astype(F32) + far.astype(F32) + near.astype(F32), late


def on_device(act_forward, weight, act_backward, pre_backward, grad_backward):
    r, x, z, y = (lax.axis_index(name) for name in ("row", "col", "z", "y"))
    ym = y % 2
    place = jnp.stack([x, r, y, z]).astype(jnp.int32)

    left, right = send(act_forward, "col", 1), send(act_forward, "col", -1)

    same = lax.dynamic_slice(act_backward, (0, ym * 1024), (64, 1024))
    other = lax.dynamic_slice(act_backward, (0, (1 - ym) * 1024), (64, 1024))
    acts = jnp.concatenate(
        [same, send(other, "y", 1), send(other, "y", -1), send(same, "y", 2)], axis=0
    )
    flipped, halves = grad_pre_flipped(pre_backward, grad_backward)

    acts, halves, flipped, left, right, act_forward = together(
        acts, halves, flipped, left, right, act_forward
    )
    far = send(act_forward, "col", 2)
    b1, b2, b3 = send(acts, "col", -1), send(acts, "col", 2), send(acts, "col", 1)
    flipped_other = send(flipped, "row", 1)
    grads_own = lax.all_to_all(halves, "y", 0, 0)
    keep, packed, *gives = both_products(
        place, (act_forward, right, far, left), flipped, flipped_other, weight
    )

    hidden_forward = gelu_rows(keep, [send(give, "row", 1) for give in gives])
    grads_own, hidden_forward, packed, b1, b2, b3 = together(
        grads_own, hidden_forward, packed, b1, b2, b3
    )
    grads_other = send(grads_own, "row", 1)
    packed = lax.all_to_all(packed, "col", 0, 0)
    parts = {}
    first = [(0, 4), (0, 3), (1, 4), (1, 5)]
    others = [(w, o) for w in range(2) for o in range(8) if (w, o) not in first]
    for wanted, late in ((first, ()), (others, ())):
        got = weight_parts(
            place, grads_own, grads_other, (acts, b1, b2, b3), wanted, wanted is first, late
        )
        parts.update(zip(wanted, got))
    given, kept = ([parts[w, o] for o in range(8)] for w in range(2))
    got, _ = reduce_z(given, -1, True)
    kept, packed = reduce_z(kept, 1, False, packed)
    grad_inputs = packed.astype(F32).sum(axis=0).astype(BF)
    grad_weight = jnp.where(
        ym == 0, jnp.concatenate([kept, got], axis=1), jnp.concatenate([got, kept], axis=1)
    ).T
    return hidden_forward, grad_inputs, grad_weight


def solution(mesh):
    fine = Mesh(mesh.devices.reshape(2, 4, 8, 4), ("row", "col", "z", "y"))
    in_specs = (
        P(("z", "y", "col"), "row"),
        P("row", "col"),
        P(("z", "y", "col"), "row"),
        P(("z", "y", "row"), "col"),
        P(("z", "y", "row"), "col"),
    )
    out_specs = (
        P(("z", "y", "row"), "col"),
        P(("z", "y", "col"), "row"),
        P("row", ("col", "z", "y")),
    )
    return jax.shard_map(
        on_device, mesh=fine, in_specs=in_specs, out_specs=out_specs, check_vma=False
    )
```

```python
import functools
import math

import jax
import jax.numpy as jnp
from jax import lax
from jax.experimental import pallas as pl
from jax.experimental.pallas import tpu as pltpu
from jax.sharding import Mesh, PartitionSpec as P

coeff = math.sqrt(2.0 / math.pi)
BF = jnp.bfloat16
F32 = jnp.float32
SIZES = {"row": 2, "col": 4, "z": 8, "y": 4}


def gelu_value(v):
    inner = coeff * (v + 0.044715 * v * v * v)
    return 0.5 * v * (1.0 + jnp.tanh(inner))


def gelu_slope(v):
    tanh_part = jnp.tanh(coeff * (v + 0.044715 * v * v * v))
    return 0.5 * (1.0 + tanh_part) + 0.5 * v * (1.0 - tanh_part * tanh_part) * coeff * (
        1.0 + 3.0 * 0.044715 * v * v
    )


def send(value, axis, step):
    n = SIZES[axis]
    return lax.ppermute(value, axis, [(i, (i + step) % n) for i in range(n)])


def together(*values):
    return lax.optimization_barrier(values)


VMEM = pl.BlockSpec(memory_space=pltpu.VMEM)
SMEM = pl.BlockSpec(memory_space=pltpu.SMEM)


def params(mib):
    return pltpu.CompilerParams(vmem_limit_bytes=mib * 2**20)


def grad_kernel(pre_ref, grad_ref, flip_ref, parts_ref):
    g = grad_ref[...].astype(F32) * gelu_slope(pre_ref[...].astype(F32))
    flip = g.T.astype(BF)
    flip_ref[...] = flip
    for k in range(4):
        for q in range(4):
            block = flip[k * 448 + q * 112 : k * 448 + q * 112 + 112]
            parts_ref[q ^ 1, 0, k * 112 : k * 112 + 112] = block
            parts_ref[q, 1, k * 112 : k * 112 + 112] = block


def grad_pre_flipped(pre, grad):
    rows, cols = pre.shape
    tile = 1792
    return pl.pallas_call(
        grad_kernel,
        grid=(cols // tile,),
        in_specs=[pl.BlockSpec((rows, tile), lambda i: (0, i))] * 2,
        out_specs=[
            pl.BlockSpec((tile, rows), lambda i: (i, 0)),
            pl.BlockSpec((4, 2, tile // 4, rows), lambda i: (0, 0, i, 0)),
        ],
        out_shape=[
            jax.ShapeDtypeStruct((cols, rows), BF),
            jax.ShapeDtypeStruct((4, 2, cols // 4, rows), BF),
        ],
        compiler_params=params(60),
        cost_estimate=pl.CostEstimate(
            flops=30 * rows * cols, bytes_accessed=10 * rows * cols, transcendentals=rows * cols
        ),
    )(pre, grad)


def copy_acts(blocks, acts, sems):
    x, r, y = (lax.axis_index(name) for name in ("col", "row", "y"))
    copies = []
    for d, block in enumerate(blocks):
        at = lax.rem(x + d, 4)
        for j, turn in enumerate((0, 3, 1, 2)):
            to = acts.at[(at // 2) ^ r, lax.rem(y + turn, 4), lax.rem(at, 2)]
            copies.append(pltpu.make_async_copy(block.at[j], to, sems.at[len(copies)]))
    return copies


def first_kernel(wanted, own_ref, oth_ref, b0, b1, b2, b3, *rest):
    outs, (acts, lhs, sems) = rest[:-3], rest[-3:]
    z = lax.axis_index("z")
    copies = copy_acts((b0, b1, b2, b3), acts, sems)
    for i, (which, offset) in enumerate(wanted):
        rows = pl.ds(pl.multiple_of(lax.rem(z + offset, 8) * 112, 16), 112)
        for h, ref in enumerate((own_ref, oth_ref)):
            to = lhs.at[pl.ds(h * 4, 4), pl.ds(i * 112, 112), :]
            sem = sems.at[len(copies)]
            copies.append(pltpu.make_async_copy(ref.at[:, which, rows, :], to, sem))
    for copy in copies:
        copy.start()
    for copy in copies:
        copy.wait()
    both = jnp.concatenate([lhs[k] for k in range(8)], axis=1)
    part = jnp.dot(both, acts[...].reshape(1024, 1024), preferred_element_type=F32)
    for i, out in enumerate(outs):
        out[...] = part[i * 112 : i * 112 + 112].astype(BF)


def rest_kernel(wanted, own_ref, oth_ref, b0, b1, b2, b3, *rest):
    outs, (acts, lhs, done, sems) = rest[:-4], rest[-4:]
    z = lax.axis_index("z")
    copies = copy_acts((b0, b1, b2, b3), acts, sems)
    for which in range(2):
        for h, ref in enumerate((own_ref, oth_ref)):
            to = lhs.at[which, pl.ds(h * 4, 4)]
            copies.append(pltpu.make_async_copy(ref.at[:, which], to, sems.at[len(copies)]))
    for copy in copies:
        copy.start()
    for copy in copies[:18]:
        copy.wait()
    sent = []
    for which in range(2):
        if which == 1:
            for copy in copies[18:]:
                copy.wait()
        mine = [(i, offset) for i, (w, offset) in enumerate(wanted) if w == which]
        pieces = []
        for _, offset in mine:
            rows = pl.ds(pl.multiple_of(lax.rem(z + offset, 8) * 112, 16), 112)
            pieces.append(jnp.concatenate([lhs[which, k, rows, :] for k in range(8)], axis=1))
        both = jnp.concatenate(pieces, axis=0)
        part = jnp.dot(both, acts[...].reshape(1024, 1024), preferred_element_type=F32)
        for k, (i, _) in enumerate(mine):
            done[i] = part[k * 112 : k * 112 + 112].astype(BF)
            sent.append(pltpu.make_async_copy(done.at[i], outs[i], sems.at[20 + i]))
            sent[-1].start()
    for copy in sent:
        copy.wait()


def weight_parts(own, oth, blocks, wanted, first):
    anywhere = pl.BlockSpec(memory_space=pl.ANY)
    n = len(wanted)
    if first:
        scratch = [pltpu.VMEM((8, 112 * n, 128), BF), pltpu.SemaphoreType.DMA((16 + 2 * n,))]
    else:
        scratch = [
            pltpu.VMEM((2, 8, 896, 128), BF),
            pltpu.VMEM((n, 112, 1024), BF),
            pltpu.SemaphoreType.DMA((20 + n,)),
        ]
    return pl.pallas_call(
        functools.partial(first_kernel if first else rest_kernel, wanted),
        grid=(1,),
        in_specs=[anywhere] * 6,
        out_specs=[pl.BlockSpec((112, 1024), lambda i: (0, 0)) if first else anywhere] * n,
        scratch_shapes=[pltpu.VMEM((2, 4, 2, 64, 1024), BF)] + scratch,
        out_shape=[jax.ShapeDtypeStruct((112, 1024), BF)] * n,
        compiler_params=params(60),
        cost_estimate=pl.CostEstimate(flops=2**20, bytes_accessed=2**20, transcendentals=0),
    )(own, oth, *(block.reshape(4, 64, 1024) for block in blocks))


def both_kernel(f0, f1, f2, f3, own_ref, oth_ref, w_ref, keep_ref, out_ref, *rest):
    gives, rows_ref, acc = rest[:-2], rest[-2], rest[-1]
    step, last = pl.program_id(0), pl.num_programs(0) - 1
    x, r = lax.axis_index("col"), lax.axis_index("row")

    @pl.when(step == 0)
    def _():
        for d, ref in enumerate((f0, f1, f2, f3)):
            at = lax.rem(x + d, 4)
            row = ((at // 2) ^ r) * 128 + lax.rem(at, 2) * 64
            rows_ref[pl.ds(pl.multiple_of(row, 64), 64), :] = ref[...]

    w = w_ref[...]
    part = jnp.dot(rows_ref[...], w, preferred_element_type=F32).astype(BF)
    keep_ref[...] = part[:128]
    for k, give in enumerate(gives):
        give[...] = part[128 + 64 * k : 192 + 64 * k]
    both = jnp.concatenate([own_ref[...], oth_ref[...]], axis=1)
    more = jnp.dot(w, both, preferred_element_type=F32)

    @pl.when(step == 0)
    def _():
        acc[...] = more

    @pl.when(step > 0)
    def _():
        acc[...] += more

    @pl.when(step == last)
    def _():
        flat = acc[...].T.astype(BF)
        for half in range(2):
            for k in range(2):
                at = (half ^ r) * 2 + k
                out_ref[at] = flat[half * 128 + k * 64 : half * 128 + k * 64 + 64]


def both_products(fwd, own, oth, weight):
    feats, hidden = weight.shape
    tile = 512
    return pl.pallas_call(
        both_kernel,
        grid=(hidden // tile,),
        in_specs=[pl.BlockSpec((64, feats), lambda i: (0, 0))] * 4
        + [pl.BlockSpec((tile, 128), lambda i: (i, 0))] * 2
        + [pl.BlockSpec((feats, tile), lambda i: (0, i))],
        out_specs=[
            pl.BlockSpec((128, tile), lambda i: (0, i)),
            pl.BlockSpec((4, 64, feats), lambda i: (0, 0, 0)),
        ]
        + [pl.BlockSpec((64, tile), lambda i: (0, i))] * 2,
        out_shape=[
            jax.ShapeDtypeStruct((128, hidden), BF),
            jax.ShapeDtypeStruct((4, 64, feats), BF),
        ]
        + [jax.ShapeDtypeStruct((64, hidden), BF)] * 2,
        scratch_shapes=[pltpu.VMEM((256, feats), BF), pltpu.VMEM((feats, 256), F32)],
        compiler_params=params(60),
        cost_estimate=pl.CostEstimate(
            flops=12 * 256 * 2048 * hidden, bytes_accessed=2 * 2048 * hidden, transcendentals=0
        ),
    )(*fwd, own, oth, weight)


def gelu_kernel(keep_ref, *refs):
    out_ref, rows = refs[-1], refs[0].shape[0]
    for k, got in enumerate(refs[:-1]):
        at = pl.ds(k * rows, rows)
        v = keep_ref[at, :].astype(F32) + got[...].astype(F32)
        out_ref[at, :] = gelu_value(v).astype(BF)


def gelu_rows(keep, got):
    rows, cols = keep.shape
    tile = 1792
    whole = pl.BlockSpec((rows, tile), lambda i: (0, i))
    return pl.pallas_call(
        gelu_kernel,
        grid=(cols // tile,),
        in_specs=[whole] + [pl.BlockSpec((rows // len(got), tile), lambda i: (0, i))] * len(got),
        out_specs=whole,
        out_shape=jax.ShapeDtypeStruct((rows, cols), BF),
        compiler_params=params(60),
        cost_estimate=pl.CostEstimate(flops=2**18, bytes_accessed=2**18, transcendentals=0),
    )(keep, *got)


def send_z(value, step, swap=False):
    pairs = []
    for k in range(8):
        for y in range(4):
            pairs.append((k * 4 + y, (k + step) % 8 * 4 + (y ^ 1 if swap else y)))
    return lax.ppermute(value, ("z", "y"), pairs)


def reduce_z(piece, step, swap, late=None):
    far, near = piece[4], piece[-3 * step % 8]
    for hop in (3, 2, 1):
        far = send_z(far, step)
        if hop == 3 and late is not None:
            far, late = together(far, late)
        near = send_z(near, -step, swap and hop == 1)
        far = far + piece[hop * step % 8]
        if hop > 1:
            near = near + piece[-(hop - 1) * step % 8]
    own = lax.ppermute(piece[0], "y", [(k, k ^ 1) for k in range(4)]) if swap else piece[0]
    far = send_z(far, step, swap)
    return own.astype(F32) + near.astype(F32) + far.astype(F32), late


def on_device(act_forward, weight, act_backward, pre_backward, grad_backward):
    r, x, z, y = (lax.axis_index(name) for name in ("row", "col", "z", "y"))
    ym = y % 2

    left, right = send(act_forward, "col", 1), send(act_forward, "col", -1)

    same = lax.dynamic_slice(act_backward, (0, ym * 1024), (64, 1024))
    other = lax.dynamic_slice(act_backward, (0, (1 - ym) * 1024), (64, 1024))
    acts = jnp.concatenate(
        [same, send(other, "y", 1), send(other, "y", -1), send(same, "y", 2)], axis=0
    )
    flipped, halves = grad_pre_flipped(pre_backward, grad_backward)

    acts, halves, flipped, left, right = together(acts, halves, flipped, left, right)
    far = send(act_forward, "col", 2)
    b1, b2, b3 = send(acts, "col", -1), send(acts, "col", 2), send(acts, "col", 1)
    flipped_other = send(flipped, "row", 1)
    grads_own = lax.all_to_all(halves, "y", 0, 0)
    keep, packed, *gives = both_products(
        (act_forward, right, far, left), flipped, flipped_other, weight
    )

    hidden_forward = gelu_rows(keep, [send(give, "row", 1) for give in gives])
    grads_own, hidden_forward, packed, b1, b2, b3 = together(
        grads_own, hidden_forward, packed, b1, b2, b3
    )
    grads_other = send(grads_own, "row", 1)
    packed = lax.all_to_all(packed, "col", 0, 0)
    parts = {}
    first = [(0, 4), (1, 4)]
    others = [(w, o) for w in range(2) for o in range(8) if (w, o) not in first]
    for wanted in (first, others):
        got = weight_parts(
            grads_own, grads_other, (acts, b1, b2, b3), wanted, wanted is first
        )
        parts.update(zip(wanted, got))
    given, kept = ([parts[w, o] for o in range(8)] for w in range(2))
    got, _ = reduce_z(given, 1, True)
    kept, packed = reduce_z(kept, -1, False, packed)
    grad_inputs = packed.astype(F32).sum(axis=0).astype(BF)
    grad_weight = jnp.where(
        ym == 0, jnp.concatenate([kept, got], axis=1), jnp.concatenate([got, kept], axis=1)
    ).T
    return hidden_forward, grad_inputs, grad_weight


def solution(mesh):
    fine = Mesh(mesh.devices.reshape(2, 4, 8, 4), ("row", "col", "z", "y"))
    in_specs = (
        P(("z", "y", "col"), "row"),
        P("row", "col"),
        P(("z", "y", "col"), "row"),
        P(("z", "y", "row"), "col"),
        P(("z", "y", "row"), "col"),
    )
    out_specs = (
        P(("z", "y", "row"), "col"),
        P(("z", "y", "col"), "row"),
        P("row", ("col", "z", "y")),
    )
    return jax.shard_map(
        on_device, mesh=fine, in_specs=in_specs, out_specs=out_specs, check_vma=False
    )
```

```python
import functools
import math

import jax
import jax.numpy as jnp
from jax import lax
from jax.experimental import pallas as pl
from jax.experimental.pallas import tpu as pltpu
from jax.sharding import Mesh, PartitionSpec as P

coeff = math.sqrt(2.0 / math.pi)
BF = jnp.bfloat16
F32 = jnp.float32
SIZES = {"row": 2, "col": 4, "z": 8, "y": 4}


def gelu_value(v):
    inner = coeff * (v + 0.044715 * v * v * v)
    return 0.5 * v * (1.0 + jnp.tanh(inner))


def gelu_slope(v):
    tanh_part = jnp.tanh(coeff * (v + 0.044715 * v * v * v))
    return 0.5 * (1.0 + tanh_part) + 0.5 * v * (1.0 - tanh_part * tanh_part) * coeff * (
        1.0 + 3.0 * 0.044715 * v * v
    )


def send(value, axis, step):
    n = SIZES[axis]
    return lax.ppermute(value, axis, [(i, (i + step) % n) for i in range(n)])


def trade(value, axis, near):
    pairs = [(i, i ^ 1 if near else (i + 2) % 4 ^ 1) for i in range(4)]
    return lax.ppermute(value, axis, pairs)


def neighbours(index):
    across = lax.rem(index + 2, 4)
    return index, index ^ 1, across, across ^ 1


def together(*values):
    return lax.optimization_barrier(values)


VMEM = pl.BlockSpec(memory_space=pltpu.VMEM)
SMEM = pl.BlockSpec(memory_space=pltpu.SMEM)


def params(mib):
    return pltpu.CompilerParams(vmem_limit_bytes=mib * 2**20)


def grad_kernel(pre_ref, grad_ref, flip_ref, parts_ref):
    g = grad_ref[...].astype(F32) * gelu_slope(pre_ref[...].astype(F32))
    flip = g.T.astype(BF)
    flip_ref[...] = flip
    for k in range(4):
        for q in range(4):
            block = flip[k * 448 + q * 112 : k * 448 + q * 112 + 112]
            parts_ref[q ^ 1, 0, k * 112 : k * 112 + 112] = block
            parts_ref[q, 1, k * 112 : k * 112 + 112] = block


def grad_pre_flipped(pre, grad):
    rows, cols = pre.shape
    tile = 1792
    return pl.pallas_call(
        grad_kernel,
        grid=(cols // tile,),
        in_specs=[pl.BlockSpec((rows, tile), lambda i: (0, i))] * 2,
        out_specs=[
            pl.BlockSpec((tile, rows), lambda i: (i, 0)),
            pl.BlockSpec((4, 2, tile // 4, rows), lambda i: (0, 0, i, 0)),
        ],
        out_shape=[
            jax.ShapeDtypeStruct((cols, rows), BF),
            jax.ShapeDtypeStruct((4, 2, cols // 4, rows), BF),
        ],
        compiler_params=params(60),
        cost_estimate=pl.CostEstimate(
            flops=30 * rows * cols, bytes_accessed=10 * rows * cols, transcendentals=rows * cols
        ),
    )(pre, grad)


def copy_acts(blocks, acts, sems):
    x, r, y = (lax.axis_index(name) for name in ("col", "row", "y"))
    copies = []
    for at, block in zip(neighbours(x), blocks):
        for j, at_y in enumerate(neighbours(y)):
            to = acts.at[(at // 2) ^ r, at_y, lax.rem(at, 2)]
            copies.append(pltpu.make_async_copy(block.at[j], to, sems.at[len(copies)]))
    return copies


def first_kernel(wanted, own_ref, oth_ref, b0, b1, b2, b3, *rest):
    outs, (acts, lhs, sems) = rest[:-3], rest[-3:]
    z = lax.axis_index("z")
    turn = 1 - 2 * lax.rem(z, 2)
    copies = copy_acts((b0, b1, b2, b3), acts, sems)
    for i, (which, offset) in enumerate(wanted):
        rows = pl.ds(pl.multiple_of(lax.rem(z + turn * offset + 8, 8) * 112, 16), 112)
        for h, ref in enumerate((own_ref, oth_ref)):
            to = lhs.at[pl.ds(h * 4, 4), pl.ds(i * 112, 112), :]
            sem = sems.at[len(copies)]
            copies.append(pltpu.make_async_copy(ref.at[:, which, rows, :], to, sem))
    for copy in copies:
        copy.start()
    for copy in copies:
        copy.wait()
    both = jnp.concatenate([lhs[k] for k in range(8)], axis=1)
    part = jnp.dot(both, acts[...].reshape(1024, 1024), preferred_element_type=F32)
    for i, out in enumerate(outs):
        out[...] = part[i * 112 : i * 112 + 112].astype(BF)


def rest_kernel(wanted, own_ref, oth_ref, b0, b1, b2, b3, *rest):
    outs, (acts, lhs, done, sems) = rest[:-4], rest[-4:]
    z = lax.axis_index("z")
    turn = 1 - 2 * lax.rem(z, 2)
    copies = copy_acts((b0, b1, b2, b3), acts, sems)
    for which in range(2):
        for h, ref in enumerate((own_ref, oth_ref)):
            to = lhs.at[which, pl.ds(h * 4, 4)]
            copies.append(pltpu.make_async_copy(ref.at[:, which], to, sems.at[len(copies)]))
    for copy in copies:
        copy.start()
    for copy in copies[:18]:
        copy.wait()
    sent = []
    for which in range(2):
        if which == 1:
            for copy in copies[18:]:
                copy.wait()
        mine = [(i, offset) for i, (w, offset) in enumerate(wanted) if w == which]
        pieces = []
        for _, offset in mine:
            rows = pl.ds(pl.multiple_of(lax.rem(z + turn * offset + 8, 8) * 112, 16), 112)
            pieces.append(jnp.concatenate([lhs[which, k, rows, :] for k in range(8)], axis=1))
        both = jnp.concatenate(pieces, axis=0)
        part = jnp.dot(both, acts[...].reshape(1024, 1024), preferred_element_type=F32)
        for k, (i, _) in enumerate(mine):
            done[i] = part[k * 112 : k * 112 + 112].astype(BF)
            sent.append(pltpu.make_async_copy(done.at[i], outs[i], sems.at[20 + i]))
            sent[-1].start()
    for copy in sent:
        copy.wait()


def weight_parts(own, oth, blocks, wanted, first):
    anywhere = pl.BlockSpec(memory_space=pl.ANY)
    n = len(wanted)
    if first:
        scratch = [pltpu.VMEM((8, 112 * n, 128), BF), pltpu.SemaphoreType.DMA((16 + 2 * n,))]
    else:
        scratch = [
            pltpu.VMEM((2, 8, 896, 128), BF),
            pltpu.VMEM((n, 112, 1024), BF),
            pltpu.SemaphoreType.DMA((20 + n,)),
        ]
    return pl.pallas_call(
        functools.partial(first_kernel if first else rest_kernel, wanted),
        grid=(1,),
        in_specs=[anywhere] * 6,
        out_specs=[pl.BlockSpec((112, 1024), lambda i: (0, 0)) if first else anywhere] * n,
        scratch_shapes=[pltpu.VMEM((2, 4, 2, 64, 1024), BF)] + scratch,
        out_shape=[jax.ShapeDtypeStruct((112, 1024), BF)] * n,
        compiler_params=params(60),
        cost_estimate=pl.CostEstimate(flops=2**20, bytes_accessed=2**20, transcendentals=0),
    )(own, oth, *(block.reshape(4, 64, 1024) for block in blocks))


def both_kernel(f0, f1, f2, f3, own_ref, oth_ref, w_ref, keep_ref, out_ref, *rest):
    gives, rows_ref, acc = rest[:-2], rest[-2], rest[-1]
    step, last = pl.program_id(0), pl.num_programs(0) - 1
    x, r = lax.axis_index("col"), lax.axis_index("row")

    @pl.when(step == 0)
    def _():
        for at, ref in zip(neighbours(x), (f0, f1, f2, f3)):
            row = ((at // 2) ^ r) * 128 + lax.rem(at, 2) * 64
            rows_ref[pl.ds(pl.multiple_of(row, 64), 64), :] = ref[...]

    w = w_ref[...]
    part = jnp.dot(rows_ref[...], w, preferred_element_type=F32).astype(BF)
    keep_ref[...] = part[:128]
    for k, give in enumerate(gives):
        give[...] = part[128 + 64 * k : 192 + 64 * k]
    both = jnp.concatenate([own_ref[...], oth_ref[...]], axis=1)
    more = jnp.dot(w, both, preferred_element_type=F32)

    @pl.when(step == 0)
    def _():
        acc[...] = more

    @pl.when(step > 0)
    def _():
        acc[...] += more

    @pl.when(step == last)
    def _():
        flat = acc[...].T.astype(BF)
        for half in range(2):
            for k in range(2):
                at = (half ^ r) * 2 + k
                out_ref[at] = flat[half * 128 + k * 64 : half * 128 + k * 64 + 64]


def both_products(fwd, own, oth, weight):
    feats, hidden = weight.shape
    tile = 512
    return pl.pallas_call(
        both_kernel,
        grid=(hidden // tile,),
        in_specs=[pl.BlockSpec((64, feats), lambda i: (0, 0))] * 4
        + [pl.BlockSpec((tile, 128), lambda i: (i, 0))] * 2
        + [pl.BlockSpec((feats, tile), lambda i: (0, i))],
        out_specs=[
            pl.BlockSpec((128, tile), lambda i: (0, i)),
            pl.BlockSpec((4, 64, feats), lambda i: (0, 0, 0)),
        ]
        + [pl.BlockSpec((64, tile), lambda i: (0, i))] * 2,
        out_shape=[
            jax.ShapeDtypeStruct((128, hidden), BF),
            jax.ShapeDtypeStruct((4, 64, feats), BF),
        ]
        + [jax.ShapeDtypeStruct((64, hidden), BF)] * 2,
        scratch_shapes=[pltpu.VMEM((256, feats), BF), pltpu.VMEM((feats, 256), F32)],
        compiler_params=params(60),
        cost_estimate=pl.CostEstimate(
            flops=12 * 256 * 2048 * hidden, bytes_accessed=2 * 2048 * hidden, transcendentals=0
        ),
    )(*fwd, own, oth, weight)


def gelu_kernel(keep_ref, *refs):
    out_ref, rows = refs[-1], refs[0].shape[0]
    for k, got in enumerate(refs[:-1]):
        at = pl.ds(k * rows, rows)
        v = keep_ref[at, :].astype(F32) + got[...].astype(F32)
        out_ref[at, :] = gelu_value(v).astype(BF)


def gelu_rows(keep, got):
    rows, cols = keep.shape
    tile = 1792
    whole = pl.BlockSpec((rows, tile), lambda i: (0, i))
    return pl.pallas_call(
        gelu_kernel,
        grid=(cols // tile,),
        in_specs=[whole] + [pl.BlockSpec((rows // len(got), tile), lambda i: (0, i))] * len(got),
        out_specs=whole,
        out_shape=jax.ShapeDtypeStruct((rows, cols), BF),
        compiler_params=params(60),
        cost_estimate=pl.CostEstimate(flops=2**18, bytes_accessed=2**18, transcendentals=0),
    )(keep, *got)


def trade_z(value, near, swap=False):
    pairs = []
    for k in range(8):
        to = k ^ 1 if near else ((k + 1) ^ 1) - 1
        for y in range(4):
            pairs.append((k * 4 + y, to % 8 * 4 + (y ^ 1 if swap else y)))
    return lax.ppermute(value, ("z", "y"), pairs)


def reduce_z(piece, near_first, swap, late=None):
    side = 1 if near_first else -1
    far, near = piece[4], piece[3 * side % 8]
    for hop in (3, 2, 1):
        by = near_first == (hop != 2)
        far = trade_z(far, by)
        if hop == 3 and late is not None:
            far, late = together(far, late)
        near = trade_z(near, by, swap and hop == 1)
        side = -side
        far = far + piece[hop * side % 8]
        if hop > 1:
            near = near + piece[(hop - 1) * side % 8]
    own = lax.ppermute(piece[0], "y", [(k, k ^ 1) for k in range(4)]) if swap else piece[0]
    far = trade_z(far, not near_first, swap)
    return (own, near, far), late


def on_device(act_forward, weight, act_backward, pre_backward, grad_backward):
    r, x, z, y = (lax.axis_index(name) for name in ("row", "col", "z", "y"))
    ym = y % 2

    left, right = trade(act_forward, "col", False), trade(act_forward, "col", True)

    same = lax.dynamic_slice(act_backward, (0, ym * 1024), (64, 1024))
    other = lax.dynamic_slice(act_backward, (0, (1 - ym) * 1024), (64, 1024))
    acts = jnp.concatenate(
        [same, trade(other, "y", True), send(same, "y", 2), trade(other, "y", False)], axis=0
    )
    flipped, halves = grad_pre_flipped(pre_backward, grad_backward)

    acts, halves, flipped, left, right = together(acts, halves, flipped, left, right)
    far = send(act_forward, "col", 2)
    b1, b2, b3 = trade(acts, "col", True), send(acts, "col", 2), trade(acts, "col", False)
    flipped_other = send(flipped, "row", 1)
    grads_own = lax.all_to_all(halves, "y", 0, 0)
    keep, packed, *gives = both_products(
        (act_forward, right, far, left), flipped, flipped_other, weight
    )

    hidden_forward = gelu_rows(keep, [send(give, "row", 1) for give in gives])
    grads_own, hidden_forward, packed, b1, b2, b3 = together(
        grads_own, hidden_forward, packed, b1, b2, b3
    )
    grads_other = send(grads_own, "row", 1)
    packed = lax.all_to_all(packed, "col", 0, 0)
    parts = {}
    first = [(0, 4), (1, 4)]
    others = [(w, o) for w in range(2) for o in range(8) if (w, o) not in first]
    for wanted in (first, others):
        got = weight_parts(
            grads_own, grads_other, (acts, b1, b2, b3), wanted, wanted is first
        )
        parts.update(zip(wanted, got))
    given, kept = ([parts[w, o] for o in range(8)] for w in range(2))
    got, _ = reduce_z(given, True, True)
    kept, packed = reduce_z(kept, False, False, packed)
    grad_inputs = packed.astype(F32).sum(axis=0).astype(BF)
    low = sum(jnp.where(ym == 0, a, b).astype(F32) for a, b in zip(kept, got))
    high = sum(jnp.where(ym == 0, b, a).astype(F32) for a, b in zip(kept, got))
    grad_weight = jnp.concatenate([low, high], axis=1).T
    return hidden_forward, grad_inputs, grad_weight


def solution(mesh):
    fine = Mesh(mesh.devices.reshape(2, 4, 8, 4), ("row", "col", "z", "y"))
    in_specs = (
        P(("z", "y", "col"), "row"),
        P("row", "col"),
        P(("z", "y", "col"), "row"),
        P(("z", "y", "row"), "col"),
        P(("z", "y", "row"), "col"),
    )
    out_specs = (
        P(("z", "y", "row"), "col"),
        P(("z", "y", "col"), "row"),
        P("row", ("col", "z", "y")),
    )
    return jax.shard_map(
        on_device, mesh=fine, in_specs=in_specs, out_specs=out_specs, check_vma=False
    )
```

```python
import functools
import math

import jax
import jax.numpy as jnp
from jax import lax
from jax.experimental import pallas as pl
from jax.experimental.pallas import tpu as pltpu
from jax.sharding import Mesh, PartitionSpec as P

coeff = math.sqrt(2.0 / math.pi)
BF = jnp.bfloat16
F32 = jnp.float32
SIZES = {"row": 2, "col": 4, "z": 8, "y": 4}


def gelu_value(v):
    inner = coeff * (v + 0.044715 * v * v * v)
    return 0.5 * v * (1.0 + jnp.tanh(inner))


def gelu_slope(v):
    tanh_part = jnp.tanh(coeff * (v + 0.044715 * v * v * v))
    return 0.5 * (1.0 + tanh_part) + 0.5 * v * (1.0 - tanh_part * tanh_part) * coeff * (
        1.0 + 3.0 * 0.044715 * v * v
    )


def send(value, axis, step):
    n = SIZES[axis]
    return lax.ppermute(value, axis, [(i, (i + step) % n) for i in range(n)])


def trade(value, axis, near):
    pairs = [(i, i ^ 1 if near else (i + 2) % 4 ^ 1) for i in range(4)]
    return lax.ppermute(value, axis, pairs)


def neighbours(index):
    across = lax.rem(index + 2, 4)
    return index, index ^ 1, across, across ^ 1


def together(*values):
    return lax.optimization_barrier(values)


VMEM = pl.BlockSpec(memory_space=pltpu.VMEM)
SMEM = pl.BlockSpec(memory_space=pltpu.SMEM)


def params(mib):
    return pltpu.CompilerParams(vmem_limit_bytes=mib * 2**20)


def grad_kernel(pre_ref, grad_ref, flip_ref, parts_ref):
    g = grad_ref[...].astype(F32) * gelu_slope(pre_ref[...].astype(F32))
    flip = g.T.astype(BF)
    flip_ref[...] = flip
    for k in range(4):
        for q in range(4):
            block = flip[k * 448 + q * 112 : k * 448 + q * 112 + 112]
            parts_ref[q ^ 1, 0, k * 112 : k * 112 + 112] = block
            parts_ref[q, 1, k * 112 : k * 112 + 112] = block


def grad_pre_flipped(pre, grad):
    rows, cols = pre.shape
    tile = 1792
    return pl.pallas_call(
        grad_kernel,
        grid=(cols // tile,),
        in_specs=[pl.BlockSpec((rows, tile), lambda i: (0, i))] * 2,
        out_specs=[
            pl.BlockSpec((tile, rows), lambda i: (i, 0)),
            pl.BlockSpec((4, 2, tile // 4, rows), lambda i: (0, 0, i, 0)),
        ],
        out_shape=[
            jax.ShapeDtypeStruct((cols, rows), BF),
            jax.ShapeDtypeStruct((4, 2, cols // 4, rows), BF),
        ],
        compiler_params=params(60),
        cost_estimate=pl.CostEstimate(
            flops=30 * rows * cols, bytes_accessed=10 * rows * cols, transcendentals=rows * cols
        ),
    )(pre, grad)


def copy_acts(blocks, acts, sems):
    x, r, y = (lax.axis_index(name) for name in ("col", "row", "y"))
    copies = []
    for at, block in zip(neighbours(x), blocks):
        for j, at_y in enumerate(neighbours(y)):
            to = acts.at[(at // 2) ^ r, at_y, lax.rem(at, 2)]
            copies.append(pltpu.make_async_copy(block.at[j], to, sems.at[len(copies)]))
    return copies


def first_kernel(wanted, own_ref, oth_ref, b0, b1, b2, b3, *rest):
    outs, (acts, lhs, sems) = rest[:-3], rest[-3:]
    z = lax.axis_index("z")
    turn = 1 - 2 * lax.rem(z, 2)
    copies = copy_acts((b0, b1, b2, b3), acts, sems)
    for i, (which, offset) in enumerate(wanted):
        rows = pl.ds(pl.multiple_of(lax.rem(z + turn * offset + 8, 8) * 112, 16), 112)
        for h, ref in enumerate((own_ref, oth_ref)):
            to = lhs.at[pl.ds(h * 4, 4), pl.ds(i * 112, 112), :]
            sem = sems.at[len(copies)]
            copies.append(pltpu.make_async_copy(ref.at[:, which, rows, :], to, sem))
    for copy in copies:
        copy.start()
    for copy in copies:
        copy.wait()
    both = jnp.concatenate([lhs[k] for k in range(8)], axis=1)
    part = jnp.dot(both, acts[...].reshape(1024, 1024), preferred_element_type=F32)
    for i, out in enumerate(outs):
        out[...] = part[i * 112 : i * 112 + 112].astype(BF)


def rest_kernel(wanted, own_ref, oth_ref, b0, b1, b2, b3, *rest):
    outs, (acts, lhs, done, sems) = rest[:-4], rest[-4:]
    z = lax.axis_index("z")
    turn = 1 - 2 * lax.rem(z, 2)
    copies = copy_acts((b0, b1, b2, b3), acts, sems)
    for which in range(2):
        for h, ref in enumerate((own_ref, oth_ref)):
            to = lhs.at[which, pl.ds(h * 4, 4)]
            copies.append(pltpu.make_async_copy(ref.at[:, which], to, sems.at[len(copies)]))
    for copy in copies:
        copy.start()
    for copy in copies[:18]:
        copy.wait()
    sent = []
    for which in range(2):
        if which == 1:
            for copy in copies[18:]:
                copy.wait()
        mine = [(i, offset) for i, (w, offset) in enumerate(wanted) if w == which]
        pieces = []
        for _, offset in mine:
            rows = pl.ds(pl.multiple_of(lax.rem(z + turn * offset + 8, 8) * 112, 16), 112)
            pieces.append(jnp.concatenate([lhs[which, k, rows, :] for k in range(8)], axis=1))
        both = jnp.concatenate(pieces, axis=0)
        part = jnp.dot(both, acts[...].reshape(1024, 1024), preferred_element_type=F32)
        for k, (i, _) in enumerate(mine):
            done[i] = part[k * 112 : k * 112 + 112].astype(BF)
            sent.append(pltpu.make_async_copy(done.at[i], outs[i], sems.at[20 + i]))
            sent[-1].start()
    for copy in sent:
        copy.wait()


def weight_parts(own, oth, blocks, wanted, first):
    anywhere = pl.BlockSpec(memory_space=pl.ANY)
    n = len(wanted)
    if first:
        scratch = [pltpu.VMEM((8, 112 * n, 128), BF), pltpu.SemaphoreType.DMA((16 + 2 * n,))]
    else:
        scratch = [
            pltpu.VMEM((2, 8, 896, 128), BF),
            pltpu.VMEM((n, 112, 1024), BF),
            pltpu.SemaphoreType.DMA((20 + n,)),
        ]
    return pl.pallas_call(
        functools.partial(first_kernel if first else rest_kernel, wanted),
        grid=(1,),
        in_specs=[anywhere] * 6,
        out_specs=[pl.BlockSpec((112, 1024), lambda i: (0, 0)) if first else anywhere] * n,
        scratch_shapes=[pltpu.VMEM((2, 4, 2, 64, 1024), BF)] + scratch,
        out_shape=[jax.ShapeDtypeStruct((112, 1024), BF)] * n,
        compiler_params=params(60),
        cost_estimate=pl.CostEstimate(flops=2**20, bytes_accessed=2**20, transcendentals=0),
    )(own, oth, *(block.reshape(4, 64, 1024) for block in blocks))


def both_kernel(f0, f1, f2, f3, own_ref, oth_ref, w_ref, keep_ref, out_ref, *rest):
    gives, rows_ref, acc = rest[:-2], rest[-2], rest[-1]
    step, last = pl.program_id(0), pl.num_programs(0) - 1
    x, r = lax.axis_index("col"), lax.axis_index("row")

    @pl.when(step == 0)
    def _():
        for at, ref in zip(neighbours(x), (f0, f1, f2, f3)):
            row = ((at // 2) ^ r) * 128 + lax.rem(at, 2) * 64
            rows_ref[pl.ds(pl.multiple_of(row, 64), 64), :] = ref[...]

    w = w_ref[...]
    part = jnp.dot(rows_ref[...], w, preferred_element_type=F32).astype(BF)
    keep_ref[...] = part[:128]
    for k, give in enumerate(gives):
        give[...] = part[128 + 64 * k : 192 + 64 * k]
    both = jnp.concatenate([own_ref[...], oth_ref[...]], axis=1)
    more = jnp.dot(w, both, preferred_element_type=F32)

    @pl.when(step == 0)
    def _():
        acc[...] = more

    @pl.when(step > 0)
    def _():
        acc[...] += more

    @pl.when(step == last)
    def _():
        flat = acc[...].T.astype(BF)
        for half in range(2):
            for k in range(2):
                at = (half ^ r) * 2 + k
                out_ref[at] = flat[half * 128 + k * 64 : half * 128 + k * 64 + 64]


def both_products(fwd, own, oth, weight):
    feats, hidden = weight.shape
    tile = 512
    return pl.pallas_call(
        both_kernel,
        grid=(hidden // tile,),
        in_specs=[pl.BlockSpec((64, feats), lambda i: (0, 0))] * 4
        + [pl.BlockSpec((tile, 128), lambda i: (i, 0))] * 2
        + [pl.BlockSpec((feats, tile), lambda i: (0, i))],
        out_specs=[
            pl.BlockSpec((128, tile), lambda i: (0, i)),
            pl.BlockSpec((4, 64, feats), lambda i: (0, 0, 0)),
        ]
        + [pl.BlockSpec((64, tile), lambda i: (0, i))] * 2,
        out_shape=[
            jax.ShapeDtypeStruct((128, hidden), BF),
            jax.ShapeDtypeStruct((4, 64, feats), BF),
        ]
        + [jax.ShapeDtypeStruct((64, hidden), BF)] * 2,
        scratch_shapes=[pltpu.VMEM((256, feats), BF), pltpu.VMEM((feats, 256), F32)],
        compiler_params=params(60),
        cost_estimate=pl.CostEstimate(
            flops=12 * 256 * 2048 * hidden, bytes_accessed=2 * 2048 * hidden, transcendentals=0
        ),
    )(*fwd, own, oth, weight)


def gelu_kernel(keep_ref, *refs):
    out_ref, rows = refs[-1], refs[0].shape[0]
    for k, got in enumerate(refs[:-1]):
        at = pl.ds(k * rows, rows)
        v = keep_ref[at, :].astype(F32) + got[...].astype(F32)
        out_ref[at, :] = gelu_value(v).astype(BF)


def gelu_rows(keep, got):
    rows, cols = keep.shape
    tile = 1792
    whole = pl.BlockSpec((rows, tile), lambda i: (0, i))
    return pl.pallas_call(
        gelu_kernel,
        grid=(cols // tile,),
        in_specs=[whole] + [pl.BlockSpec((rows // len(got), tile), lambda i: (0, i))] * len(got),
        out_specs=whole,
        out_shape=jax.ShapeDtypeStruct((rows, cols), BF),
        compiler_params=params(60),
        cost_estimate=pl.CostEstimate(flops=2**18, bytes_accessed=2**18, transcendentals=0),
    )(keep, *got)


def trade_z(value, near, swap=False):
    pairs = []
    for k in range(8):
        to = k ^ 1 if near else ((k + 1) ^ 1) - 1
        for y in range(4):
            pairs.append((k * 4 + y, to % 8 * 4 + (y ^ 1 if swap else y)))
    return lax.ppermute(value, ("z", "y"), pairs)


def reduce_z(piece, near_first, swap, late=None):
    side = 1 if near_first else -1
    far, near = piece[4], piece[3 * side % 8]
    for hop in (3, 2, 1):
        by = near_first == (hop != 2)
        far = trade_z(far, by)
        if hop == 3 and late is not None:
            far, late = together(far, late)
        near = trade_z(near, by, swap and hop == 1)
        side = -side
        far = far + piece[hop * side % 8]
        if hop > 1:
            near = near + piece[(hop - 1) * side % 8]
    own = lax.ppermute(piece[0], "y", [(k, k ^ 1) for k in range(4)]) if swap else piece[0]
    far = trade_z(far, not near_first, swap)
    return (own, near, far), late


def on_device(act_forward, weight, act_backward, pre_backward, grad_backward):
    r, x, z, y = (lax.axis_index(name) for name in ("row", "col", "z", "y"))
    ym = y % 2

    left, right = trade(act_forward, "col", False), trade(act_forward, "col", True)

    same = lax.dynamic_slice(act_backward, (0, ym * 1024), (64, 1024))
    other = lax.dynamic_slice(act_backward, (0, (1 - ym) * 1024), (64, 1024))
    acts = jnp.concatenate(
        [same, trade(other, "y", True), send(same, "y", 2), trade(other, "y", False)], axis=0
    )
    flipped, halves = grad_pre_flipped(pre_backward, grad_backward)

    acts, halves, flipped, left, right = together(acts, halves, flipped, left, right)
    far = send(act_forward, "col", 2)
    b1, b2, b3 = trade(acts, "col", True), send(acts, "col", 2), trade(acts, "col", False)
    flipped_other = send(flipped, "row", 1)
    grads_own = lax.all_to_all(halves, "y", 0, 0)
    keep, packed, *gives = both_products(
        (act_forward, right, far, left), flipped, flipped_other, weight
    )

    hidden_forward = gelu_rows(keep, [send(give, "row", 1) for give in gives])
    grads_own, hidden_forward, packed, b1, b2, b3 = together(
        grads_own, hidden_forward, packed, b1, b2, b3
    )
    grads_other = send(grads_own, "row", 1)
    packed = lax.all_to_all(packed, "col", 0, 0)
    parts = {}
    first = [(0, 4), (1, 4), (0, 3), (1, 5)]
    others = [(w, o) for w in range(2) for o in range(8) if (w, o) not in first]
    for wanted in (first, others):
        got = weight_parts(
            grads_own, grads_other, (acts, b1, b2, b3), wanted, wanted is first
        )
        parts.update(zip(wanted, got))
    given, kept = ([parts[w, o] for o in range(8)] for w in range(2))
    got, _ = reduce_z(given, True, True)
    kept, packed = reduce_z(kept, False, False, packed)
    grad_inputs = packed.astype(F32).sum(axis=0).astype(BF)
    low = sum(jnp.where(ym == 0, a, b).astype(F32) for a, b in zip(kept, got))
    high = sum(jnp.where(ym == 0, b, a).astype(F32) for a, b in zip(kept, got))
    grad_weight = jnp.concatenate([low, high], axis=1).T
    return hidden_forward, grad_inputs, grad_weight


def solution(mesh):
    fine = Mesh(mesh.devices.reshape(2, 4, 8, 4), ("row", "col", "z", "y"))
    in_specs = (
        P(("z", "y", "col"), "row"),
        P("row", "col"),
        P(("z", "y", "col"), "row"),
        P(("z", "y", "row"), "col"),
        P(("z", "y", "row"), "col"),
    )
    out_specs = (
        P(("z", "y", "row"), "col"),
        P(("z", "y", "col"), "row"),
        P("row", ("col", "z", "y")),
    )
    return jax.shard_map(
        on_device, mesh=fine, in_specs=in_specs, out_specs=out_specs, check_vma=False
    )
```

```python
import functools
import math

import jax
import jax.numpy as jnp
from jax import lax
from jax.experimental import pallas as pl
from jax.experimental.pallas import tpu as pltpu
from jax.sharding import Mesh, PartitionSpec as P

coeff = math.sqrt(2.0 / math.pi)
BF = jnp.bfloat16
F32 = jnp.float32
SIZES = {"row": 2, "col": 4, "z": 8, "y": 4}


def gelu_value(v):
    inner = coeff * (v + 0.044715 * v * v * v)
    return 0.5 * v * (1.0 + jnp.tanh(inner))


def gelu_slope(v):
    tanh_part = jnp.tanh(coeff * (v + 0.044715 * v * v * v))
    return 0.5 * (1.0 + tanh_part) + 0.5 * v * (1.0 - tanh_part * tanh_part) * coeff * (
        1.0 + 3.0 * 0.044715 * v * v
    )


def send(value, axis, step):
    n = SIZES[axis]
    return lax.ppermute(value, axis, [(i, (i + step) % n) for i in range(n)])


def trade(value, axis, near):
    pairs = [(i, i ^ 1 if near else (i + 2) % 4 ^ 1) for i in range(4)]
    return lax.ppermute(value, axis, pairs)


def neighbours(index):
    across = lax.rem(index + 2, 4)
    return index, index ^ 1, across, across ^ 1


def together(*values):
    return lax.optimization_barrier(values)


VMEM = pl.BlockSpec(memory_space=pltpu.VMEM)
SMEM = pl.BlockSpec(memory_space=pltpu.SMEM)


def params(mib):
    return pltpu.CompilerParams(vmem_limit_bytes=mib * 2**20)


def grad_kernel(pre_ref, grad_ref, flip_ref, parts_ref):
    g = grad_ref[...].astype(F32) * gelu_slope(pre_ref[...].astype(F32))
    flip = g.T.astype(BF)
    flip_ref[...] = flip
    for k in range(4):
        for q in range(4):
            block = flip[k * 448 + q * 112 : k * 448 + q * 112 + 112]
            parts_ref[q ^ 1, 0, k * 112 : k * 112 + 112] = block
            parts_ref[q, 1, k * 112 : k * 112 + 112] = block


def grad_pre_flipped(pre, grad):
    rows, cols = pre.shape
    tile = 1792
    return pl.pallas_call(
        grad_kernel,
        grid=(cols // tile,),
        in_specs=[pl.BlockSpec((rows, tile), lambda i: (0, i))] * 2,
        out_specs=[
            pl.BlockSpec((tile, rows), lambda i: (i, 0)),
            pl.BlockSpec((4, 2, tile // 4, rows), lambda i: (0, 0, i, 0)),
        ],
        out_shape=[
            jax.ShapeDtypeStruct((cols, rows), BF),
            jax.ShapeDtypeStruct((4, 2, cols // 4, rows), BF),
        ],
        compiler_params=params(60),
        cost_estimate=pl.CostEstimate(
            flops=30 * rows * cols, bytes_accessed=10 * rows * cols, transcendentals=rows * cols
        ),
    )(pre, grad)


def copy_acts(blocks, acts, sems):
    x, r, y = (lax.axis_index(name) for name in ("col", "row", "y"))
    copies = []
    for at, block in zip(neighbours(x), blocks):
        for j, at_y in enumerate(neighbours(y)):
            to = acts.at[(at // 2) ^ r, at_y, lax.rem(at, 2)]
            copies.append(pltpu.make_async_copy(block.at[j], to, sems.at[len(copies)]))
    return copies


def first_kernel(wanted, own_ref, oth_ref, b0, b1, b2, b3, *rest):
    outs, (acts, lhs, sems) = rest[:-3], rest[-3:]
    z = lax.axis_index("z")
    turn = 1 - 2 * lax.rem(z, 2)
    copies = copy_acts((b0, b1, b2, b3), acts, sems)
    for i, (which, offset) in enumerate(wanted):
        rows = pl.ds(pl.multiple_of(lax.rem(z + turn * offset + 8, 8) * 112, 16), 112)
        for h, ref in enumerate((own_ref, oth_ref)):
            to = lhs.at[pl.ds(h * 4, 4), pl.ds(i * 112, 112), :]
            sem = sems.at[len(copies)]
            copies.append(pltpu.make_async_copy(ref.at[:, which, rows, :], to, sem))
    for copy in copies:
        copy.start()
    for copy in copies:
        copy.wait()
    both = jnp.concatenate([lhs[k] for k in range(8)], axis=1)
    part = jnp.dot(both, acts[...].reshape(1024, 1024), preferred_element_type=F32)
    for i, out in enumerate(outs):
        out[...] = part[i * 112 : i * 112 + 112].astype(BF)


def rest_kernel(wanted, own_ref, oth_ref, b0, b1, b2, b3, *rest):
    outs, (acts, lhs, done, sems) = rest[:-4], rest[-4:]
    z = lax.axis_index("z")
    turn = 1 - 2 * lax.rem(z, 2)
    copies = copy_acts((b0, b1, b2, b3), acts, sems)
    for which in range(2):
        for h, ref in enumerate((own_ref, oth_ref)):
            to = lhs.at[which, pl.ds(h * 4, 4)]
            copies.append(pltpu.make_async_copy(ref.at[:, which], to, sems.at[len(copies)]))
    for copy in copies:
        copy.start()
    for copy in copies[:18]:
        copy.wait()
    sent = []
    for which in range(2):
        if which == 1:
            for copy in copies[18:]:
                copy.wait()
        mine = [(i, offset) for i, (w, offset) in enumerate(wanted) if w == which]
        pieces = []
        for _, offset in mine:
            rows = pl.ds(pl.multiple_of(lax.rem(z + turn * offset + 8, 8) * 112, 16), 112)
            pieces.append(jnp.concatenate([lhs[which, k, rows, :] for k in range(8)], axis=1))
        both = jnp.concatenate(pieces, axis=0)
        part = jnp.dot(both, acts[...].reshape(1024, 1024), preferred_element_type=F32)
        for k, (i, _) in enumerate(mine):
            done[i] = part[k * 112 : k * 112 + 112].astype(BF)
            sent.append(pltpu.make_async_copy(done.at[i], outs[i], sems.at[20 + i]))
            sent[-1].start()
    for copy in sent:
        copy.wait()


def weight_parts(own, oth, blocks, wanted, first):
    anywhere = pl.BlockSpec(memory_space=pl.ANY)
    n = len(wanted)
    if first:
        scratch = [pltpu.VMEM((8, 112 * n, 128), BF), pltpu.SemaphoreType.DMA((16 + 2 * n,))]
    else:
        scratch = [
            pltpu.VMEM((2, 8, 896, 128), BF),
            pltpu.VMEM((n, 112, 1024), BF),
            pltpu.SemaphoreType.DMA((20 + n,)),
        ]
    return pl.pallas_call(
        functools.partial(first_kernel if first else rest_kernel, wanted),
        grid=(1,),
        in_specs=[anywhere] * 6,
        out_specs=[pl.BlockSpec((112, 1024), lambda i: (0, 0)) if first else anywhere] * n,
        scratch_shapes=[pltpu.VMEM((2, 4, 2, 64, 1024), BF)] + scratch,
        out_shape=[jax.ShapeDtypeStruct((112, 1024), BF)] * n,
        compiler_params=params(60),
        cost_estimate=pl.CostEstimate(flops=2**20, bytes_accessed=2**20, transcendentals=0),
    )(own, oth, *(block.reshape(4, 64, 1024) for block in blocks))


def both_kernel(f0, f1, f2, f3, own_ref, oth_ref, w_ref, keep_ref, out_ref, *rest):
    gives, rows_ref, acc = rest[:-2], rest[-2], rest[-1]
    step, last = pl.program_id(0), pl.num_programs(0) - 1
    x, r = lax.axis_index("col"), lax.axis_index("row")

    @pl.when(step == 0)
    def _():
        for at, ref in zip(neighbours(x), (f0, f1, f2, f3)):
            row = ((at // 2) ^ r) * 128 + lax.rem(at, 2) * 64
            rows_ref[pl.ds(pl.multiple_of(row, 64), 64), :] = ref[...]

    w = w_ref[...]
    part = jnp.dot(rows_ref[...], w, preferred_element_type=F32).astype(BF)
    keep_ref[...] = part[:128]
    for k, give in enumerate(gives):
        give[...] = part[128 + 64 * k : 192 + 64 * k]
    both = jnp.concatenate([own_ref[...], oth_ref[...]], axis=1)
    more = jnp.dot(w, both, preferred_element_type=F32)

    @pl.when(step == 0)
    def _():
        acc[...] = more

    @pl.when(step > 0)
    def _():
        acc[...] += more

    @pl.when(step == last)
    def _():
        flat = acc[...].T.astype(BF)
        for half in range(2):
            for k in range(2):
                at = (half ^ r) * 2 + k
                out_ref[at] = flat[half * 128 + k * 64 : half * 128 + k * 64 + 64]


def both_products(fwd, own, oth, weight):
    feats, hidden = weight.shape
    tile = 512
    return pl.pallas_call(
        both_kernel,
        grid=(hidden // tile,),
        in_specs=[pl.BlockSpec((64, feats), lambda i: (0, 0))] * 4
        + [pl.BlockSpec((tile, 128), lambda i: (i, 0))] * 2
        + [pl.BlockSpec((feats, tile), lambda i: (0, i))],
        out_specs=[
            pl.BlockSpec((128, tile), lambda i: (0, i)),
            pl.BlockSpec((4, 64, feats), lambda i: (0, 0, 0)),
        ]
        + [pl.BlockSpec((64, tile), lambda i: (0, i))] * 2,
        out_shape=[
            jax.ShapeDtypeStruct((128, hidden), BF),
            jax.ShapeDtypeStruct((4, 64, feats), BF),
        ]
        + [jax.ShapeDtypeStruct((64, hidden), BF)] * 2,
        scratch_shapes=[pltpu.VMEM((256, feats), BF), pltpu.VMEM((feats, 256), F32)],
        compiler_params=params(60),
        cost_estimate=pl.CostEstimate(
            flops=12 * 256 * 2048 * hidden, bytes_accessed=2 * 2048 * hidden, transcendentals=0
        ),
    )(*fwd, own, oth, weight)


def gelu_kernel(keep_ref, *refs):
    out_ref, rows = refs[-1], refs[0].shape[0]
    for k, got in enumerate(refs[:-1]):
        at = pl.ds(k * rows, rows)
        v = keep_ref[at, :].astype(F32) + got[...].astype(F32)
        out_ref[at, :] = gelu_value(v).astype(BF)


def gelu_rows(keep, got):
    rows, cols = keep.shape
    tile = 1792
    whole = pl.BlockSpec((rows, tile), lambda i: (0, i))
    return pl.pallas_call(
        gelu_kernel,
        grid=(cols // tile,),
        in_specs=[whole] + [pl.BlockSpec((rows // len(got), tile), lambda i: (0, i))] * len(got),
        out_specs=whole,
        out_shape=jax.ShapeDtypeStruct((rows, cols), BF),
        compiler_params=params(60),
        cost_estimate=pl.CostEstimate(flops=2**18, bytes_accessed=2**18, transcendentals=0),
    )(keep, *got)


def trade_z(value, near, swap=False):
    pairs = []
    for k in range(8):
        to = k ^ 1 if near else ((k + 1) ^ 1) - 1
        for y in range(4):
            pairs.append((k * 4 + y, to % 8 * 4 + (y ^ 1 if swap else y)))
    return lax.ppermute(value, ("z", "y"), pairs)


def reduce_z(piece, near_first, swap, late=None):
    side = 1 if near_first else -1
    far, near = piece[4], piece[3 * side % 8]
    for hop in (3, 2, 1):
        by = near_first == (hop != 2)
        far = trade_z(far, by)
        if hop == 3 and late is not None:
            far, late = together(far, late)
        near = trade_z(near, by, swap and hop == 1)
        side = -side
        far = far + piece[hop * side % 8]
        if hop > 1:
            near = near + piece[(hop - 1) * side % 8]
    own = lax.ppermute(piece[0], "y", [(k, k ^ 1) for k in range(4)]) if swap else piece[0]
    far = trade_z(far, not near_first, swap)
    return (own, near, far), late


def on_device(act_forward, weight, act_backward, pre_backward, grad_backward):
    r, x, z, y = (lax.axis_index(name) for name in ("row", "col", "z", "y"))
    ym = y % 2

    left, right = trade(act_forward, "col", False), trade(act_forward, "col", True)

    same = lax.dynamic_slice(act_backward, (0, ym * 1024), (64, 1024))
    other = lax.dynamic_slice(act_backward, (0, (1 - ym) * 1024), (64, 1024))
    acts = jnp.concatenate(
        [same, trade(other, "y", True), send(same, "y", 2), trade(other, "y", False)], axis=0
    )
    flipped, halves = grad_pre_flipped(pre_backward, grad_backward)

    acts, halves, flipped, left, right = together(acts, halves, flipped, left, right)
    far = send(act_forward, "col", 2)
    b1, b2, b3 = trade(acts, "col", True), send(acts, "col", 2), trade(acts, "col", False)
    flipped_other = send(flipped, "row", 1)
    grads_own = lax.all_to_all(halves, "y", 0, 0)
    keep, packed, *gives = both_products(
        (act_forward, right, far, left), flipped, flipped_other, weight
    )

    hidden_forward = gelu_rows(keep, [send(give, "row", 1) for give in gives])
    grads_own, hidden_forward, packed, b1, b2, b3 = together(
        grads_own, hidden_forward, packed, b1, b2, b3
    )
    grads_other = send(grads_own, "row", 1)
    packed = lax.all_to_all(packed, "col", 0, 0)
    parts = {}
    first = [(0, 4), (1, 4), (0, 3), (1, 5)]
    others = [(w, o) for w in range(2) for o in range(8) if (w, o) not in first]
    for wanted in (first, others):
        got = weight_parts(
            grads_own, grads_other, (acts, b1, b2, b3), wanted, wanted is first
        )
        parts.update(zip(wanted, got))
    given, kept = ([parts[w, o] for o in range(8)] for w in range(2))
    got, packed = reduce_z(given, True, True, packed)
    kept, _ = reduce_z(kept, False, False)
    grad_inputs = packed.astype(F32).sum(axis=0).astype(BF)
    low = sum(jnp.where(ym == 0, a, b).astype(F32) for a, b in zip(kept, got))
    high = sum(jnp.where(ym == 0, b, a).astype(F32) for a, b in zip(kept, got))
    grad_weight = jnp.concatenate([low, high], axis=1).T
    return hidden_forward, grad_inputs, grad_weight


def solution(mesh):
    fine = Mesh(mesh.devices.reshape(2, 4, 8, 4), ("row", "col", "z", "y"))
    in_specs = (
        P(("z", "y", "col"), "row"),
        P("row", "col"),
        P(("z", "y", "col"), "row"),
        P(("z", "y", "row"), "col"),
        P(("z", "y", "row"), "col"),
    )
    out_specs = (
        P(("z", "y", "row"), "col"),
        P(("z", "y", "col"), "row"),
        P("row", ("col", "z", "y")),
    )
    return jax.shard_map(
        on_device, mesh=fine, in_specs=in_specs, out_specs=out_specs, check_vma=False
    )
```
